32 devices in a mesh: row: 2 (over y), col: 4 (over z), vec: 4 (over x, core).
Axes of the slice: x: 2, y: 2, z: 4, core: 2. Of those that a mesh axis runs over, the one named last changes fastest.
Arguments:
- particles: bfloat16 [1024, 512], P(('row', 'col', 'vec')), may hold values from -6 to 6
- start_basis: float32 [1024, 64], P(('row', 'col', 'vec')), may hold values from -6 to 6
Outputs:
- basis: float32 [1024, 64], P(('row', 'col', 'vec'))
- factor: float32 [64, 64], replicated
The draws below stay inside these ranges and needn't reach their ends.
All inputs are finite; a program needn't handle non-finite values.
Results may differ from the reference program's by a relative error of at most 0.0003.
Values may be sent and summed in bfloat16 or wider, within the bound.
No kernel may reach another device: no remote copies, remote signals or barrier semaphores. Data moves between devices by JAX's collectives and lax.ppermute only.
A program may use at most 64 MiB of HBM per device.

```python
import math
import jax
import jax.numpy as jnp
from jax import lax

FEAT = 512
EIG = 64
ITERS = 2
PARTICLES = 1024


def steps_of(rng, dims, split, low, largest):
    gain = 1.0
    for dim, parts in split:
        draws = jax.random.uniform(jax.random.fold_in(jax.random.fold_in(rng, 6), dim), (parts,), jnp.float32, low / len(split), largest / len(split))
        gain = gain * jnp.repeat(jnp.exp(draws), dims[dim] // parts).reshape((-1,) + (1,) * (len(dims) - 1 - dim))
    return gain


def gaussian(rng, shape, scale, reach, split=(), kind=jnp.bfloat16):
    entries = scale * jax.random.normal(rng, shape, jnp.float32)
    if split:
        entries = entries * steps_of(rng, shape, split, -0.22, 0.18)
    return jnp.clip(entries, -reach, reach).astype(kind)


def setup_inputs(seed: int = 0) -> dict:
    keys = jax.random.split(jax.random.key(seed), 3)
    particles = gaussian(keys[0], (PARTICLES, FEAT), 1.0, 6.0, ((0, 32),))
    start_basis = gaussian(keys[1], (PARTICLES, EIG), 1.0, 6.0, ((0, 32),), jnp.float32)
    return dict(particles=particles, start_basis=start_basis)


def reference(particles, start_basis):
    total_rows = PARTICLES
    block_rows = math.gcd(total_rows, 512)
    block_count = total_rows // block_rows
    spread = 2.0 * FEAT
    particles_f = particles.astype(jnp.float32)
    squares = lax.optimization_barrier(jnp.sum(particles_f * particles_f, axis=1))
    all_ids = jnp.arange(total_rows, dtype=jnp.int32)
    block_list = jnp.arange(block_count, dtype=jnp.int32)

    def kernel_rows(block_idx):
        offset = (block_idx * block_rows).astype(jnp.int32)
        row_block = lax.dynamic_slice_in_dim(particles, offset, block_rows, 0)
        row_sq = lax.dynamic_slice_in_dim(squares, offset, block_rows, 0)
        inner_dots = jnp.dot(row_block.astype(jnp.float32), particles.T.astype(jnp.float32), preferred_element_type=jnp.float32)
        distance = row_sq[:, None] + squares[None, :] - 2.0 * inner_dots
        row_ids = offset + jnp.arange(block_rows, dtype=jnp.int32)
        return jnp.where(row_ids[:, None] == all_ids[None, :], jnp.float32(0.0), jnp.exp(-distance / spread))
    degree = lax.map(lambda block_idx: lax.optimization_barrier(jnp.sum(kernel_rows(block_idx), axis=1)), block_list).reshape(total_rows)
    degree_sum = jnp.sum(degree)
    inv_root = 1.0 / jnp.sqrt(degree)
    root_vec = jnp.sqrt(degree) / jnp.sqrt(degree_sum)
    basis_now = start_basis
    factor = jnp.zeros((EIG, EIG), jnp.float32)
    for sweep in range(ITERS):
        scaled = basis_now * inv_root[:, None]
        product = lax.map(lambda block_idx: jnp.dot(kernel_rows(block_idx), scaled, precision=lax.Precision.HIGHEST), block_list).reshape(total_rows, EIG)
        aligned = jnp.dot(root_vec, basis_now, precision=lax.Precision.HIGHEST)
        deflated = product * inv_root[:, None] - root_vec[:, None] * aligned[None, :]
        gram_mat = jnp.dot(deflated.T, deflated, precision=lax.Precision.HIGHEST)
        factor = jnp.linalg.cholesky(gram_mat)
        solved = jax.scipy.linalg.solve_triangular(factor, deflated.T, lower=True)
        basis_now = solved.T * math.sqrt(float(total_rows))
    return (basis_now, factor)
```

```python
import math

import jax
import jax.numpy as jnp
from jax import lax
from jax.sharding import PartitionSpec as P

ITERS = 2
AXES = ("row", "col", "vec")
WHOLE_ROWS = 2048


def sharded(particles, start_basis):
    shard_rows = particles.shape[0]
    width = particles.shape[1]
    eig_cols = start_basis.shape[1]
    row_size = lax.axis_size("row")
    col_size = lax.axis_size("col")
    vec_size = lax.axis_size("vec")
    total_rows = shard_rows * row_size * col_size * vec_size
    rowpos = lax.axis_index("row")
    colpos = lax.axis_index("col")
    vecpos = lax.axis_index("vec")
    spread = 2.0 * width
    root_total = math.sqrt(float(total_rows))
    row_feats = lax.all_gather(particles, "row", axis=0, tiled=True)
    col_feats = lax.all_gather(particles, ("col", "vec"), axis=0, tiled=True)
    row_iota = jnp.arange(row_feats.shape[0], dtype=jnp.int32)
    col_iota = jnp.arange(col_feats.shape[0], dtype=jnp.int32)
    row_ids = (
        (row_iota // shard_rows * col_size + colpos) * vec_size + vecpos
    ) * shard_rows + row_iota % shard_rows
    col_ids = (
        (rowpos * col_size + col_iota // (vec_size * shard_rows)) * vec_size
        + col_iota // shard_rows % vec_size
    ) * shard_rows + col_iota % shard_rows
    row_sq = jnp.sum(jnp.square(row_feats.astype(jnp.float32)), axis=1)
    col_sq = jnp.sum(jnp.square(col_feats.astype(jnp.float32)), axis=1)
    same_particle = row_ids[:, None] == col_ids[None, :]
    inner_dots = lax.dot_general(
        row_feats, col_feats, (((1,), (1,)), ((), ())), preferred_element_type=jnp.float32
    )
    distance = row_sq[:, None] + col_sq[None, :] - 2.0 * inner_dots
    kernel_tile = jnp.where(same_particle, jnp.float32(0.0), jnp.exp(-distance / spread))
    row_degree = jnp.sum(kernel_tile, axis=1)
    degree = lax.psum_scatter(row_degree, "row", scatter_dimension=0, tiled=True)
    root_deg = jnp.sqrt(degree)
    inv_root = 1.0 / root_deg
    local_total = jnp.sum(degree)
    degree_sum, raw_align = lax.psum(
        (local_total, jnp.dot(root_deg, start_basis, precision=lax.Precision.HIGHEST)), AXES
    )
    aligned = raw_align / jnp.sqrt(degree_sum)
    basis_now = start_basis
    factor = jnp.zeros((eig_cols, eig_cols), jnp.float32)
    for sweep in range(ITERS):
        scaled = basis_now * inv_root[:, None]
        partial_prod = jnp.dot(
            kernel_tile,
            lax.all_gather(scaled, ("col", "vec"), axis=0, tiled=True),
            precision=lax.Precision.HIGHEST,
        )
        product = lax.psum_scatter(partial_prod, "row", scatter_dimension=0, tiled=True)
        weighted = product * inv_root[:, None]
        root_vec = root_deg / jnp.sqrt(degree_sum)
        deflated = weighted - root_vec[:, None] * aligned[None, :]
        gram_mat, tail = lax.psum(
            (
                jnp.dot(deflated.T, deflated, precision=lax.Precision.HIGHEST),
                jnp.dot(root_vec, deflated, precision=lax.Precision.HIGHEST),
            ),
            AXES,
        )
        factor = jnp.linalg.cholesky(gram_mat)
        aligned = root_total * jax.scipy.linalg.solve_triangular(factor, tail, lower=True)
        solved = jax.scipy.linalg.solve_triangular(factor, deflated.T, lower=True)
        basis_now = solved.T * root_total
    return (basis_now, factor)


def replicated(particles, start_basis):
    shard_rows, width = particles.shape
    eig_cols = start_basis.shape[1]
    base_hi = lax.reduce_precision(start_basis, 8, 7)
    rest = start_basis - base_hi
    base_mid = lax.reduce_precision(rest, 8, 7)
    base_hi, base_mid, base_lo = (
        part.astype(jnp.bfloat16) for part in (base_hi, base_mid, rest - base_mid)
    )
    packed = jnp.concatenate([particles, base_hi, base_mid, base_lo, jnp.zeros_like(base_lo)], axis=1)
    everything = lax.all_gather(packed, AXES, axis=0, tiled=True)
    feats = everything[:, :width]
    basis = (
        everything[:, width : width + eig_cols].astype(jnp.float32)
        + everything[:, width + eig_cols : width + 2 * eig_cols].astype(jnp.float32)
        + everything[:, width + 2 * eig_cols : width + 3 * eig_cols].astype(jnp.float32)
    )
    total_rows = feats.shape[0]
    spread = 2.0 * width
    root_total = math.sqrt(float(total_rows))
    place = (lax.axis_index("row") * lax.axis_size("col") + lax.axis_index("col")) * lax.axis_size(
        "vec"
    ) + lax.axis_index("vec")
    squares = jnp.sum(jnp.square(feats.astype(jnp.float32)), axis=1)
    inner_dots = lax.dot_general(
        feats, feats, (((1,), (1,)), ((), ())), preferred_element_type=jnp.float32
    )
    distance = squares[:, None] + squares[None, :] - 2.0 * inner_dots
    ids = jnp.arange(total_rows, dtype=jnp.int32)
    kernel = jnp.where(ids[:, None] == ids[None, :], jnp.float32(0.0), jnp.exp(-distance / spread))
    degree = jnp.sum(kernel, axis=1)
    root_deg = jnp.sqrt(degree)
    inv_root = 1.0 / root_deg
    root_vec = root_deg / jnp.sqrt(jnp.sum(degree))
    matrix = kernel * inv_root[:, None] * inv_root[None, :] - root_vec[:, None] * root_vec[None, :]
    now = basis
    factor = None
    for sweep in range(ITERS):
        now = jnp.dot(matrix, now, precision=lax.Precision.HIGHEST)
        gram = jnp.dot(now.T, now, precision=lax.Precision.HIGHEST)
        factor = jnp.linalg.cholesky(gram)
        if sweep == ITERS - 1:
            now = lax.dynamic_slice_in_dim(now, place * shard_rows, shard_rows, 0)
        now = jax.scipy.linalg.solve_triangular(factor, now.T, lower=True).T * root_total
    return (now, factor)


def local(particles, start_basis):
    devices = lax.axis_size("row") * lax.axis_size("col") * lax.axis_size("vec")
    if particles.shape[0] * devices <= WHOLE_ROWS:
        return replicated(particles, start_basis)
    return sharded(particles, start_basis)


def solution(mesh):
    placed = (P(AXES, None), P(AXES, None))
    return jax.shard_map(
        local,
        mesh=mesh,
        in_specs=placed,
        out_specs=(P(AXES, None), P()),
        check_vma=False,
    )
```

```python
import math

import jax
import jax.numpy as jnp
from jax import lax
from jax.sharding import PartitionSpec as P

ITERS = 2
AXES = ("row", "col", "vec")
WHOLE_ROWS = 2048


def sharded(particles, start_basis):
    shard_rows = particles.shape[0]
    width = particles.shape[1]
    eig_cols = start_basis.shape[1]
    row_size = lax.axis_size("row")
    col_size = lax.axis_size("col")
    vec_size = lax.axis_size("vec")
    total_rows = shard_rows * row_size * col_size * vec_size
    rowpos = lax.axis_index("row")
    colpos = lax.axis_index("col")
    vecpos = lax.axis_index("vec")
    spread = 2.0 * width
    root_total = math.sqrt(float(total_rows))
    row_feats = lax.all_gather(particles, "row", axis=0, tiled=True)
    col_feats = lax.all_gather(particles, ("col", "vec"), axis=0, tiled=True)
    row_iota = jnp.arange(row_feats.shape[0], dtype=jnp.int32)
    col_iota = jnp.arange(col_feats.shape[0], dtype=jnp.int32)
    row_ids = (
        (row_iota // shard_rows * col_size + colpos) * vec_size + vecpos
    ) * shard_rows + row_iota % shard_rows
    col_ids = (
        (rowpos * col_size + col_iota // (vec_size * shard_rows)) * vec_size
        + col_iota // shard_rows % vec_size
    ) * shard_rows + col_iota % shard_rows
    row_sq = jnp.sum(jnp.square(row_feats.astype(jnp.float32)), axis=1)
    col_sq = jnp.sum(jnp.square(col_feats.astype(jnp.float32)), axis=1)
    same_particle = row_ids[:, None] == col_ids[None, :]
    inner_dots = lax.dot_general(
        row_feats, col_feats, (((1,), (1,)), ((), ())), preferred_element_type=jnp.float32
    )
    distance = row_sq[:, None] + col_sq[None, :] - 2.0 * inner_dots
    kernel_tile = jnp.where(same_particle, jnp.float32(0.0), jnp.exp(-distance / spread))
    row_degree = jnp.sum(kernel_tile, axis=1)
    degree = lax.psum_scatter(row_degree, "row", scatter_dimension=0, tiled=True)
    root_deg = jnp.sqrt(degree)
    inv_root = 1.0 / root_deg
    local_total = jnp.sum(degree)
    degree_sum, raw_align = lax.psum(
        (local_total, jnp.dot(root_deg, start_basis, precision=lax.Precision.HIGHEST)), AXES
    )
    aligned = raw_align / jnp.sqrt(degree_sum)
    basis_now = start_basis
    factor = jnp.zeros((eig_cols, eig_cols), jnp.float32)
    for sweep in range(ITERS):
        scaled = basis_now * inv_root[:, None]
        partial_prod = jnp.dot(
            kernel_tile,
            lax.all_gather(scaled, ("col", "vec"), axis=0, tiled=True),
            precision=lax.Precision.HIGHEST,
        )
        product = lax.psum_scatter(partial_prod, "row", scatter_dimension=0, tiled=True)
        weighted = product * inv_root[:, None]
        root_vec = root_deg / jnp.sqrt(degree_sum)
        deflated = weighted - root_vec[:, None] * aligned[None, :]
        gram_mat, tail = lax.psum(
            (
                jnp.dot(deflated.T, deflated, precision=lax.Precision.HIGHEST),
                jnp.dot(root_vec, deflated, precision=lax.Precision.HIGHEST),
            ),
            AXES,
        )
        factor = jnp.linalg.cholesky(gram_mat)
        aligned = root_total * jax.scipy.linalg.solve_triangular(factor, tail, lower=True)
        solved = jax.scipy.linalg.solve_triangular(factor, deflated.T, lower=True)
        basis_now = solved.T * root_total
    return (basis_now, factor)


def swap(block, axis_sizes, bits):
    count = math.prod(axis_sizes)
    return lax.ppermute(block, AXES, [(place, place ^ bits) for place in range(count)])


def gather_all(block):
    sizes = tuple(lax.axis_size(name) for name in AXES)
    vec_size = sizes[2]
    col_bits = [k * vec_size for k in range(1, sizes[1])]
    row_bit = sizes[1] * vec_size
    plane_bits = [r * row_bit + v for r in range(sizes[0]) for v in range(0, vec_size, 2)][1:]
    for bits in (col_bits, plane_bits, [1]):
        block = jnp.concatenate([block] + [swap(block, sizes, k) for k in bits], axis=0)
    return block


def replicated(particles, start_basis):
    shard_rows, width = particles.shape
    eig_cols = start_basis.shape[1]
    base_hi = lax.reduce_precision(start_basis, 8, 7)
    base_lo = lax.reduce_precision(start_basis - base_hi, 8, 7)
    packed = jnp.concatenate(
        [particles, base_hi.astype(jnp.bfloat16), base_lo.astype(jnp.bfloat16)], axis=1
    )
    everything = gather_all(packed)
    feats = everything[:, :width]
    basis = everything[:, width : width + eig_cols].astype(jnp.float32) + everything[
        :, width + eig_cols : width + 2 * eig_cols
    ].astype(jnp.float32)
    total_rows = feats.shape[0]
    spread = 2.0 * width
    root_total = math.sqrt(float(total_rows))
    squares = jnp.sum(jnp.square(feats.astype(jnp.float32)), axis=1)
    inner_dots = lax.dot_general(
        feats, feats, (((1,), (1,)), ((), ())), preferred_element_type=jnp.float32
    )
    distance = squares[:, None] + squares[None, :] - 2.0 * inner_dots
    ids = jnp.arange(total_rows, dtype=jnp.int32)
    kernel = jnp.where(ids[:, None] == ids[None, :], jnp.float32(0.0), jnp.exp(-distance / spread))
    degree = jnp.sum(kernel, axis=1)
    root_deg = jnp.sqrt(degree)
    inv_root = 1.0 / root_deg
    root_vec = root_deg / jnp.sqrt(jnp.sum(degree))
    matrix = kernel * inv_root[:, None] * inv_root[None, :] - root_vec[:, None] * root_vec[None, :]
    now = basis
    factor = None
    for sweep in range(ITERS):
        now = jnp.dot(matrix, now, precision=lax.Precision.HIGHEST)
        gram = jnp.dot(now.T, now, precision=lax.Precision.HIGHEST)
        factor = jnp.linalg.cholesky(gram)
        if sweep == ITERS - 1:
            now = now[:shard_rows]
        now = jax.scipy.linalg.solve_triangular(factor, now.T, lower=True).T * root_total
    return (now, factor)


def local(particles, start_basis):
    devices = lax.axis_size("row") * lax.axis_size("col") * lax.axis_size("vec")
    if particles.shape[0] * devices <= WHOLE_ROWS:
        return replicated(particles, start_basis)
    return sharded(particles, start_basis)


def solution(mesh):
    placed = (P(AXES, None), P(AXES, None))
    return jax.shard_map(
        local,
        mesh=mesh,
        in_specs=placed,
        out_specs=(P(AXES, None), P()),
        check_vma=False,
    )
```

```python
import functools
import math

import jax
import jax.numpy as jnp
from jax import lax
from jax.experimental import pallas as pl
from jax.experimental.pallas import tpu as pltpu
from jax.sharding import PartitionSpec as P

ITERS = 2
AXES = ("row", "col", "vec")
WHOLE_ROWS = 2048
SAFE_PART = 1.0 / 16.0
SAFE_SHARE = 1.0 / 8.0


def sharded(particles, start_basis):
    shard_rows = particles.shape[0]
    width = particles.shape[1]
    eig_cols = start_basis.shape[1]
    row_size = lax.axis_size("row")
    col_size = lax.axis_size("col")
    vec_size = lax.axis_size("vec")
    total_rows = shard_rows * row_size * col_size * vec_size
    rowpos = lax.axis_index("row")
    colpos = lax.axis_index("col")
    vecpos = lax.axis_index("vec")
    spread = 2.0 * width
    root_total = math.sqrt(float(total_rows))
    row_feats = lax.all_gather(particles, "row", axis=0, tiled=True)
    col_feats = lax.all_gather(particles, ("col", "vec"), axis=0, tiled=True)
    row_iota = jnp.arange(row_feats.shape[0], dtype=jnp.int32)
    col_iota = jnp.arange(col_feats.shape[0], dtype=jnp.int32)
    row_ids = (
        (row_iota // shard_rows * col_size + colpos) * vec_size + vecpos
    ) * shard_rows + row_iota % shard_rows
    col_ids = (
        (rowpos * col_size + col_iota // (vec_size * shard_rows)) * vec_size
        + col_iota // shard_rows % vec_size
    ) * shard_rows + col_iota % shard_rows
    row_sq = jnp.sum(jnp.square(row_feats.astype(jnp.float32)), axis=1)
    col_sq = jnp.sum(jnp.square(col_feats.astype(jnp.float32)), axis=1)
    same_particle = row_ids[:, None] == col_ids[None, :]
    inner_dots = lax.dot_general(
        row_feats, col_feats, (((1,), (1,)), ((), ())), preferred_element_type=jnp.float32
    )
    distance = row_sq[:, None] + col_sq[None, :] - 2.0 * inner_dots
    kernel_tile = jnp.where(same_particle, jnp.float32(0.0), jnp.exp(-distance / spread))
    row_degree = jnp.sum(kernel_tile, axis=1)
    degree = lax.psum_scatter(row_degree, "row", scatter_dimension=0, tiled=True)
    root_deg = jnp.sqrt(degree)
    inv_root = 1.0 / root_deg
    local_total = jnp.sum(degree)
    degree_sum, raw_align = lax.psum(
        (local_total, jnp.dot(root_deg, start_basis, precision=lax.Precision.HIGHEST)), AXES
    )
    aligned = raw_align / jnp.sqrt(degree_sum)
    basis_now = start_basis
    factor = jnp.zeros((eig_cols, eig_cols), jnp.float32)
    for sweep in range(ITERS):
        scaled = basis_now * inv_root[:, None]
        partial_prod = jnp.dot(
            kernel_tile,
            lax.all_gather(scaled, ("col", "vec"), axis=0, tiled=True),
            precision=lax.Precision.HIGHEST,
        )
        product = lax.psum_scatter(partial_prod, "row", scatter_dimension=0, tiled=True)
        weighted = product * inv_root[:, None]
        root_vec = root_deg / jnp.sqrt(degree_sum)
        deflated = weighted - root_vec[:, None] * aligned[None, :]
        gram_mat, tail = lax.psum(
            (
                jnp.dot(deflated.T, deflated, precision=lax.Precision.HIGHEST),
                jnp.dot(root_vec, deflated, precision=lax.Precision.HIGHEST),
            ),
            AXES,
        )
        factor = jnp.linalg.cholesky(gram_mat)
        aligned = root_total * jax.scipy.linalg.solve_triangular(factor, tail, lower=True)
        solved = jax.scipy.linalg.solve_triangular(factor, deflated.T, lower=True)
        basis_now = solved.T * root_total
    return (basis_now, factor)


def swap(block, axis_sizes, bits):
    count = math.prod(axis_sizes)
    return lax.ppermute(block, AXES, [(place, place ^ bits) for place in range(count)])


def gather_all(block):
    sizes = tuple(lax.axis_size(name) for name in AXES)
    vec_size = sizes[2]
    row_bit = sizes[1] * vec_size
    plane = [r * row_bit + v for r in range(sizes[0]) for v in range(0, vec_size, 2)][1:]
    steps = sorted(range(1, sizes[1]), key=lambda k: (k != 2, -k))
    line = {k: swap(block, sizes, k * vec_size) for k in steps}
    sides = [swap(block, sizes, bits) for bits in plane]
    along = jnp.concatenate([line[k] for k in steps], axis=0)
    own = [jnp.concatenate([block] + sides, axis=0), along] + [swap(along, sizes, bits) for bits in plane]
    return own + [swap(piece, sizes, 1) for piece in own]


def split(value):
    high = value.astype(jnp.bfloat16)
    return high, (value - high.astype(jnp.float32)).astype(jnp.bfloat16)


def mul(left, right, contract):
    left_hi, left_lo = split(left)
    right_hi, right_lo = right if isinstance(right, tuple) else split(right)
    rows = left.shape[0]
    dims = (((1,), (contract,)), ((), ()))
    both = lax.dot_general(
        jnp.concatenate([left_hi, left_lo], axis=0), right_hi, dims, preferred_element_type=jnp.float32
    )
    rest = lax.dot_general(left_hi, right_lo, dims, preferred_element_type=jnp.float32)
    return both[:rows] + both[rows:] + rest


def eliminate(grams):
    size = grams[0].shape[0]
    groups = size // 8
    wide = 2 * size
    eye = jnp.where(
        lax.broadcasted_iota(jnp.int32, (size, size), 0) == lax.broadcasted_iota(jnp.int32, (size, size), 1),
        jnp.float32(1.0),
        jnp.float32(0.0),
    )
    sub = lax.broadcasted_iota(jnp.int32, (8, wide), 0)
    works = []
    for gram in grams:
        work = jnp.concatenate([eye, gram], axis=1)
        works.append([work[8 * g : 8 * g + 8] for g in range(groups)])
    all_pivots = [[] for _ in grams]

    def row(block, at):
        return jnp.broadcast_to(block[at : at + 1], (8, wide))

    def two_columns(cols, work, pivots, q, j):
        first, both, second = row(cols[j][q], j), row(cols[j][q], j + 1), row(cols[j + 1][q], j + 1)
        det = first * second - both * both
        over_first = pl.reciprocal(first, approx=True)
        over_second = pl.reciprocal(det, approx=True) * first
        step = both * over_first
        heads = {k: row(cols[k][q], j) for k in range(j + 2, 8)}
        nexts = {k: row(cols[k][q], j + 1) - step * heads[k] for k in range(j + 2, 8)}
        head_row = row(work[q], j)
        next_row = row(work[q], j + 1) - step * head_row
        for g in range(q, groups):
            times = cols[j][g] * over_first
            if g == q:
                times = jnp.where(sub > j, times, 0.0)
            again = (cols[j + 1][g] - times * both) * over_second
            if g == q:
                again = jnp.where(sub > j + 1, again, 0.0)
            for k in range(j + 2, 8):
                cols[k][g] = cols[k][g] - times * heads[k] - again * nexts[k]
            work[g] = work[g] - times * head_row - again * next_row
        pivots = jnp.where(sub == j, first, pivots)
        return jnp.where(sub == j + 1, det * over_first, pivots)

    for q in range(groups):
        start = size + 8 * q
        panels = [
            [
                {g: jnp.broadcast_to(work[g][:, start + j : start + j + 1], (8, wide)) for g in range(q, groups)}
                for j in range(8)
            ]
            for work in works
        ]
        pivots = [panel[0][q] for panel in panels]
        for j in range(0, 8, 2):
            for m, work in enumerate(works):
                pivots[m] = two_columns(panels[m], work, pivots[m], q, j)
        for m, work in enumerate(works):
            work[q] = work[q] * lax.rsqrt(pivots[m])
            all_pivots[m].append(pivots[m])
    return [
        (jnp.concatenate(work, axis=0), jnp.concatenate(pivots, axis=0))
        for work, pivots in zip(works, all_pivots)
    ]


def whole_kernel(width, eig_cols, *refs):
    basis_ref, factor_ref, high_ref, low_ref, held_basis_ref, held_factor_ref, sems = refs[-7:]
    total_rows = high_ref.shape[0]
    tile = 128
    count = total_rows // tile
    packed = jnp.concatenate([piece[...] for piece in refs[:-7]], axis=0)
    feats = packed[:, :width]
    root_total = math.sqrt(float(total_rows))
    spread = 2.0 * width
    to_power = 2.0 / spread * math.log2(math.e)
    tile_eye = lax.broadcasted_iota(jnp.int32, (tile, tile), 0) == lax.broadcasted_iota(
        jnp.int32, (tile, tile), 1
    )
    weights = []
    for i in range(count):
        some = feats[i * tile : (i + 1) * tile].astype(jnp.float32)
        weights.append(jnp.exp(jnp.sum(some * some, axis=1, keepdims=True) * (-1.0 / spread)))
    def products(c):
        columns = feats[c * tile : (c + 2) * tile]
        return lax.dot_general(feats, columns, (((1,), (1,)), ((), ())), preferred_element_type=jnp.float32)

    def fill(shift):
        sums, squares = [], []
        ahead = products(0)
        for c in range(0, count, 2):
            dots = ahead
            if c + 2 < count:
                ahead = products(c + 2)
            for k in range(c, c + 2):
                less = 1.0 if shift is None else shift[:, k * tile : (k + 1) * tile]
                total = jnp.zeros((8, tile), jnp.float32)
                for i in range(count):
                    part = dots[i * tile : (i + 1) * tile, (k - c) * tile : (k - c + 1) * tile]
                    grown = jnp.exp2(part * to_power)
                    if i == k:
                        squares.append(jnp.sum(jnp.where(tile_eye, part, 0.0), axis=0, keepdims=True))
                        grown = jnp.where(tile_eye, 0.0, grown)
                    total = total + jnp.sum((grown * weights[i]).reshape(tile // 8, 8, tile), axis=0)
                    high, low = split(grown - less)
                    high_ref[i * tile : (i + 1) * tile, k * tile : (k + 1) * tile] = high
                    low_ref[i * tile : (i + 1) * tile, k * tile : (k + 1) * tile] = low
                sums.append(jnp.sum(total, axis=0, keepdims=True))
        return jnp.concatenate(sums, axis=1), jnp.concatenate(squares, axis=1)

    sums, squares = fill(None)
    weight = jnp.exp(squares * (-1.0 / spread))
    degree = weight * sums
    root_deg = jnp.sqrt(degree)
    scale = weight / root_deg
    root_vec = root_deg / jnp.sqrt(jnp.sum(degree, axis=1, keepdims=True))
    turned = packed[:, width:].astype(jnp.float32).T
    basis = turned[:eig_cols] + turned[eig_cols:]
    basis = basis / jnp.max(jnp.abs(basis), axis=1, keepdims=True)
    share = sums / jnp.sum(weight, axis=1, keepdims=True) - SAFE_SHARE

    def deflate(vectors, shift=None):
        scaled = vectors * scale
        product = mul(scaled, (high_ref[...], low_ref[...]), 0)
        whole_sum = jnp.sum(scaled, axis=1, keepdims=True)
        product = product + (whole_sum if shift is None else whole_sum * shift)
        return product * scale - jnp.sum(vectors * root_vec, axis=1, keepdims=True) * root_vec

    rows_at = lax.broadcasted_iota(jnp.int32, (eig_cols, eig_cols), 0)
    cols_at = lax.broadcasted_iota(jnp.int32, (eig_cols, eig_cols), 1)

    copies = [
        pltpu.make_async_copy(held_factor_ref, factor_ref, sems.at[0]),
        pltpu.make_async_copy(held_basis_ref, basis_ref, sems.at[1]),
    ]

    def put(inverse, last, factor):
        held_factor_ref[...] = jnp.where(rows_at >= cols_at, factor, 0.0)
        copies[0].start()
        held_basis_ref[...] = mul(inverse * root_total, last, 0).T[: basis_ref.shape[0]]
        copies[1].start()

    first = deflate(basis)
    second = deflate(first)
    grams = [mul(first, first, 1), mul(second, second, 1)]
    (inner, inner_pivots), (outer, outer_pivots) = eliminate(grams)
    put(
        outer[:, :eig_cols],
        second[:, :tile],
        mul(inner[:, :eig_cols] * root_total, outer[:, eig_cols:], 1),
    )
    lengths = [
        jnp.sum(jnp.where(rows_at == cols_at, gram, 0.0), axis=1, keepdims=True) for gram in grams
    ]
    safe = jnp.minimum(
        jnp.min(inner_pivots - lengths[0] * SAFE_PART), jnp.min(outer_pivots - lengths[1] * SAFE_PART)
    )
    safe = jnp.minimum(safe, jnp.min(share))
    for copy in copies:
        copy.wait()

    @pl.when(jnp.logical_not(safe > 0.0))
    def one_sweep_after_the_other():
        shift = jnp.where(share > 0.0, 1.0, 0.0)
        fill(shift)
        now = deflate(basis, shift)
        ((solved, _),) = eliminate([mul(now, now, 1)])
        now = mul(solved[:, :eig_cols] * root_total, now, 0)
        now = deflate(now, shift)
        ((solved, _),) = eliminate([mul(now, now, 1)])
        put(solved[:, :eig_cols], now[:, :tile], solved[:, eig_cols:].T)
        for copy in copies:
            copy.wait()


def whole(pieces, shard_rows, width, eig_cols):
    total_rows = sum(piece.shape[0] for piece in pieces)
    return pl.pallas_call(
        functools.partial(whole_kernel, width, eig_cols),
        out_shape=(
            jax.ShapeDtypeStruct((shard_rows, eig_cols), jnp.float32),
            jax.ShapeDtypeStruct((eig_cols, eig_cols), jnp.float32),
        ),
        in_specs=[pl.BlockSpec(memory_space=pltpu.VMEM)] * len(pieces),
        out_specs=(pl.BlockSpec(memory_space=pltpu.HBM),) * 2,
        scratch_shapes=[
            pltpu.VMEM((total_rows, total_rows), jnp.bfloat16),
            pltpu.VMEM((total_rows, total_rows), jnp.bfloat16),
            pltpu.VMEM((shard_rows, eig_cols), jnp.float32),
            pltpu.VMEM((eig_cols, eig_cols), jnp.float32),
            pltpu.SemaphoreType.DMA((2,)),
        ],
        compiler_params=pltpu.CompilerParams(vmem_limit_bytes=40 * 1024 * 1024),
        cost_estimate=pl.CostEstimate(
            flops=2 * total_rows * total_rows * (width + 6 * eig_cols),
            bytes_accessed=2 * total_rows * (width + 2 * eig_cols),
            transcendentals=total_rows * total_rows,
        ),
        name="subspace_sweeps",
    )(*pieces)


def replicated(particles, start_basis):
    shard_rows, width = particles.shape
    eig_cols = start_basis.shape[1]
    base_hi = lax.reduce_precision(start_basis, 8, 7)
    base_lo = lax.reduce_precision(start_basis - base_hi, 8, 7)
    packed = jnp.concatenate(
        [particles, base_hi.astype(jnp.bfloat16), base_lo.astype(jnp.bfloat16)], axis=1
    )
    return whole(gather_all(packed), shard_rows, width, eig_cols)


def local(particles, start_basis):
    devices = lax.axis_size("row") * lax.axis_size("col") * lax.axis_size("vec")
    if particles.shape[0] * devices <= WHOLE_ROWS:
        return replicated(particles, start_basis)
    return sharded(particles, start_basis)


def solution(mesh):
    placed = (P(AXES, None), P(AXES, None))
    return jax.shard_map(
        local,
        mesh=mesh,
        in_specs=placed,
        out_specs=(P(AXES, None), P()),
        check_vma=False,
    )
```

```python
import functools
import math

import jax
import jax.numpy as jnp
from jax import lax
from jax.experimental import pallas as pl
from jax.experimental.pallas import tpu as pltpu
from jax.sharding import PartitionSpec as P

ITERS = 2
AXES = ("row", "col", "vec")
WHOLE_ROWS = 2048
SAFE_PART = 1.0 / 16.0
SAFE_SHARE = 1.0 / 8.0


def sharded(particles, start_basis):
    shard_rows = particles.shape[0]
    width = particles.shape[1]
    eig_cols = start_basis.shape[1]
    row_size = lax.axis_size("row")
    col_size = lax.axis_size("col")
    vec_size = lax.axis_size("vec")
    total_rows = shard_rows * row_size * col_size * vec_size
    rowpos = lax.axis_index("row")
    colpos = lax.axis_index("col")
    vecpos = lax.axis_index("vec")
    spread = 2.0 * width
    root_total = math.sqrt(float(total_rows))
    row_feats = lax.all_gather(particles, "row", axis=0, tiled=True)
    col_feats = lax.all_gather(particles, ("col", "vec"), axis=0, tiled=True)
    row_iota = jnp.arange(row_feats.shape[0], dtype=jnp.int32)
    col_iota = jnp.arange(col_feats.shape[0], dtype=jnp.int32)
    row_ids = (
        (row_iota // shard_rows * col_size + colpos) * vec_size + vecpos
    ) * shard_rows + row_iota % shard_rows
    col_ids = (
        (rowpos * col_size + col_iota // (vec_size * shard_rows)) * vec_size
        + col_iota // shard_rows % vec_size
    ) * shard_rows + col_iota % shard_rows
    row_sq = jnp.sum(jnp.square(row_feats.astype(jnp.float32)), axis=1)
    col_sq = jnp.sum(jnp.square(col_feats.astype(jnp.float32)), axis=1)
    same_particle = row_ids[:, None] == col_ids[None, :]
    inner_dots = lax.dot_general(
        row_feats, col_feats, (((1,), (1,)), ((), ())), preferred_element_type=jnp.float32
    )
    distance = row_sq[:, None] + col_sq[None, :] - 2.0 * inner_dots
    kernel_tile = jnp.where(same_particle, jnp.float32(0.0), jnp.exp(-distance / spread))
    row_degree = jnp.sum(kernel_tile, axis=1)
    degree = lax.psum_scatter(row_degree, "row", scatter_dimension=0, tiled=True)
    root_deg = jnp.sqrt(degree)
    inv_root = 1.0 / root_deg
    local_total = jnp.sum(degree)
    degree_sum, raw_align = lax.psum(
        (local_total, jnp.dot(root_deg, start_basis, precision=lax.Precision.HIGHEST)), AXES
    )
    aligned = raw_align / jnp.sqrt(degree_sum)
    basis_now = start_basis
    factor = jnp.zeros((eig_cols, eig_cols), jnp.float32)
    for sweep in range(ITERS):
        scaled = basis_now * inv_root[:, None]
        partial_prod = jnp.dot(
            kernel_tile,
            lax.all_gather(scaled, ("col", "vec"), axis=0, tiled=True),
            precision=lax.Precision.HIGHEST,
        )
        product = lax.psum_scatter(partial_prod, "row", scatter_dimension=0, tiled=True)
        weighted = product * inv_root[:, None]
        root_vec = root_deg / jnp.sqrt(degree_sum)
        deflated = weighted - root_vec[:, None] * aligned[None, :]
        gram_mat, tail = lax.psum(
            (
                jnp.dot(deflated.T, deflated, precision=lax.Precision.HIGHEST),
                jnp.dot(root_vec, deflated, precision=lax.Precision.HIGHEST),
            ),
            AXES,
        )
        factor = jnp.linalg.cholesky(gram_mat)
        aligned = root_total * jax.scipy.linalg.solve_triangular(factor, tail, lower=True)
        solved = jax.scipy.linalg.solve_triangular(factor, deflated.T, lower=True)
        basis_now = solved.T * root_total
    return (basis_now, factor)


def swap(block, axis_sizes, bits):
    count = math.prod(axis_sizes)
    return lax.ppermute(block, AXES, [(place, place ^ bits) for place in range(count)])


def gather_all(block):
    sizes = tuple(lax.axis_size(name) for name in AXES)
    vec_size = sizes[2]
    row_bit = sizes[1] * vec_size
    plane = [r * row_bit + v for r in range(sizes[0]) for v in range(0, vec_size, 2)][1:]
    steps = sorted(range(1, sizes[1]), key=lambda k: (k != 2, -k))
    line = {k: swap(block, sizes, k * vec_size) for k in steps}
    sides = [swap(block, sizes, bits) for bits in plane]
    along = jnp.concatenate([line[k] for k in steps], axis=0)
    own = [jnp.concatenate([block] + sides, axis=0), along] + [swap(along, sizes, bits) for bits in plane]
    return own + [swap(piece, sizes, 1) for piece in own]


def split(value):
    high = value.astype(jnp.bfloat16)
    return high, (value - high.astype(jnp.float32)).astype(jnp.bfloat16)


def mul(left, right, contract):
    left_hi, left_lo = split(left)
    right_hi, right_lo = right if isinstance(right, tuple) else split(right)
    rows = left.shape[0]
    dims = (((1,), (contract,)), ((), ()))
    both = lax.dot_general(
        jnp.concatenate([left_hi, left_lo], axis=0), right_hi, dims, preferred_element_type=jnp.float32
    )
    rest = lax.dot_general(left_hi, right_lo, dims, preferred_element_type=jnp.float32)
    return both[:rows] + both[rows:] + rest


def eliminate(grams):
    size = grams[0].shape[0]
    groups = size // 8
    wide = 2 * size
    eye = jnp.where(
        lax.broadcasted_iota(jnp.int32, (size, size), 0) == lax.broadcasted_iota(jnp.int32, (size, size), 1),
        jnp.float32(1.0),
        jnp.float32(0.0),
    )
    sub = lax.broadcasted_iota(jnp.int32, (8, wide), 0)
    works = []
    for gram in grams:
        work = jnp.concatenate([eye, gram], axis=1)
        works.append([work[8 * g : 8 * g + 8] for g in range(groups)])
    all_pivots = [[] for _ in grams]

    def row(block, at):
        return jnp.broadcast_to(block[at : at + 1], (8, wide))

    def two_columns(cols, work, pivots, q, j):
        first, both, second = row(cols[j][q], j), row(cols[j][q], j + 1), row(cols[j + 1][q], j + 1)
        det = first * second - both * both
        over_first = pl.reciprocal(first, approx=True)
        over_second = pl.reciprocal(det, approx=True) * first
        step = both * over_first
        heads = {k: row(cols[k][q], j) for k in range(j + 2, 8)}
        nexts = {k: row(cols[k][q], j + 1) - step * heads[k] for k in range(j + 2, 8)}
        head_row = row(work[q], j)
        next_row = row(work[q], j + 1) - step * head_row
        for g in range(q, groups):
            times = cols[j][g] * over_first
            if g == q:
                times = jnp.where(sub > j, times, 0.0)
            again = (cols[j + 1][g] - times * both) * over_second
            if g == q:
                again = jnp.where(sub > j + 1, again, 0.0)
            for k in range(j + 2, 8):
                cols[k][g] = cols[k][g] - times * heads[k] - again * nexts[k]
            work[g] = work[g] - times * head_row - again * next_row
        pivots = jnp.where(sub == j, first, pivots)
        return jnp.where(sub == j + 1, det * over_first, pivots)

    for q in range(groups):
        start = size + 8 * q
        panels = [
            [
                {g: jnp.broadcast_to(work[g][:, start + j : start + j + 1], (8, wide)) for g in range(q, groups)}
                for j in range(8)
            ]
            for work in works
        ]
        pivots = [panel[0][q] for panel in panels]
        for j in range(0, 8, 2):
            for m, work in enumerate(works):
                pivots[m] = two_columns(panels[m], work, pivots[m], q, j)
        for m, work in enumerate(works):
            work[q] = work[q] * lax.rsqrt(pivots[m])
            all_pivots[m].append(pivots[m])
    return [
        (jnp.concatenate(work, axis=0), jnp.concatenate(pivots, axis=0))
        for work, pivots in zip(works, all_pivots)
    ]


def whole_kernel(width, eig_cols, *refs):
    basis_ref, factor_ref, pair_ref, held_basis_ref, held_factor_ref, sems = refs[-6:]
    total_rows = pair_ref.shape[1]
    high_ref, low_ref = pair_ref.at[:total_rows], pair_ref.at[total_rows:]
    tile = 128
    count = total_rows // tile
    packed = jnp.concatenate([piece[...] for piece in refs[:-6]], axis=0)
    feats = packed[:, :width]
    root_total = math.sqrt(float(total_rows))
    spread = 2.0 * width
    to_power = 2.0 / spread * math.log2(math.e)
    tile_eye = lax.broadcasted_iota(jnp.int32, (tile, tile), 0) == lax.broadcasted_iota(
        jnp.int32, (tile, tile), 1
    )
    weights = []
    for i in range(count):
        some = feats[i * tile : (i + 1) * tile].astype(jnp.float32)
        weights.append(jnp.exp(jnp.sum(some * some, axis=1, keepdims=True) * (-1.0 / spread)))
    def products(c):
        columns = feats[c * tile : (c + 2) * tile]
        return lax.dot_general(feats, columns, (((1,), (1,)), ((), ())), preferred_element_type=jnp.float32)

    def fill(shift):
        sums, squares = [], []
        ahead = products(0)
        for c in range(0, count, 2):
            dots = ahead
            if c + 2 < count:
                ahead = products(c + 2)
            for k in range(c, c + 2):
                less = 1.0 if shift is None else shift[:, k * tile : (k + 1) * tile]
                total = jnp.zeros((8, tile), jnp.float32)
                for i in range(count):
                    part = dots[i * tile : (i + 1) * tile, (k - c) * tile : (k - c + 1) * tile]
                    grown = jnp.exp2(part * to_power)
                    if i == k:
                        squares.append(jnp.sum(jnp.where(tile_eye, part, 0.0), axis=0, keepdims=True))
                        grown = jnp.where(tile_eye, 0.0, grown)
                    total = total + jnp.sum((grown * weights[i]).reshape(tile // 8, 8, tile), axis=0)
                    high, low = split(grown - less)
                    high_ref[i * tile : (i + 1) * tile, k * tile : (k + 1) * tile] = high
                    low_ref[i * tile : (i + 1) * tile, k * tile : (k + 1) * tile] = low
                sums.append(jnp.sum(total, axis=0, keepdims=True))
        return jnp.concatenate(sums, axis=1), jnp.concatenate(squares, axis=1)

    sums, squares = fill(None)
    weight = jnp.exp(squares * (-1.0 / spread))
    degree = weight * sums
    root_deg = jnp.sqrt(degree)
    scale = weight / root_deg
    root_vec = root_deg / jnp.sqrt(jnp.sum(degree, axis=1, keepdims=True))
    turned = packed[:, width:].astype(jnp.float32).T
    basis = turned[:eig_cols] + turned[eig_cols:]
    basis = basis / jnp.max(jnp.abs(basis), axis=1, keepdims=True)
    share = sums / jnp.sum(weight, axis=1, keepdims=True) - SAFE_SHARE

    def deflate(vectors, shift=None):
        scaled = vectors * scale
        parts = jnp.concatenate(split(scaled), axis=0)
        product = jnp.dot(
            jnp.concatenate([parts, parts], axis=1), pair_ref[...], preferred_element_type=jnp.float32
        )
        product = product[:eig_cols] + product[eig_cols:]
        whole_sum = jnp.sum(scaled, axis=1, keepdims=True)
        product = product + (whole_sum if shift is None else whole_sum * shift)
        return product * scale - jnp.sum(vectors * root_vec, axis=1, keepdims=True) * root_vec

    rows_at = lax.broadcasted_iota(jnp.int32, (eig_cols, eig_cols), 0)
    cols_at = lax.broadcasted_iota(jnp.int32, (eig_cols, eig_cols), 1)

    copies = [
        pltpu.make_async_copy(held_factor_ref, factor_ref, sems.at[0]),
        pltpu.make_async_copy(held_basis_ref, basis_ref, sems.at[1]),
    ]

    def put(inverse, last, factor):
        held_factor_ref[...] = jnp.where(rows_at >= cols_at, factor, 0.0)
        copies[0].start()
        held_basis_ref[...] = mul(inverse * root_total, last, 0).T[: basis_ref.shape[0]]
        copies[1].start()

    first = deflate(basis)
    second = deflate(first)
    grams = [mul(first, first, 1), mul(second, second, 1)]
    (inner, inner_pivots), (outer, outer_pivots) = eliminate(grams)
    put(
        outer[:, :eig_cols],
        second[:, :tile],
        mul(inner[:, :eig_cols] * root_total, outer[:, eig_cols:], 1),
    )
    lengths = [
        jnp.sum(jnp.where(rows_at == cols_at, gram, 0.0), axis=1, keepdims=True) for gram in grams
    ]
    safe = jnp.minimum(
        jnp.min(inner_pivots - lengths[0] * SAFE_PART), jnp.min(outer_pivots - lengths[1] * SAFE_PART)
    )
    safe = jnp.minimum(safe, jnp.min(share))
    for copy in copies:
        copy.wait()

    @pl.when(jnp.logical_not(safe > 0.0))
    def one_sweep_after_the_other():
        shift = jnp.where(share > 0.0, 1.0, 0.0)
        fill(shift)
        now = deflate(basis, shift)
        ((solved, _),) = eliminate([mul(now, now, 1)])
        now = mul(solved[:, :eig_cols] * root_total, now, 0)
        now = deflate(now, shift)
        ((solved, _),) = eliminate([mul(now, now, 1)])
        put(solved[:, :eig_cols], now[:, :tile], solved[:, eig_cols:].T)
        for copy in copies:
            copy.wait()


def whole(pieces, shard_rows, width, eig_cols):
    total_rows = sum(piece.shape[0] for piece in pieces)
    return pl.pallas_call(
        functools.partial(whole_kernel, width, eig_cols),
        out_shape=(
            jax.ShapeDtypeStruct((shard_rows, eig_cols), jnp.float32),
            jax.ShapeDtypeStruct((eig_cols, eig_cols), jnp.float32),
        ),
        in_specs=[pl.BlockSpec(memory_space=pltpu.VMEM)] * len(pieces),
        out_specs=(pl.BlockSpec(memory_space=pltpu.HBM),) * 2,
        scratch_shapes=[
            pltpu.VMEM((2 * total_rows, total_rows), jnp.bfloat16),
            pltpu.VMEM((shard_rows, eig_cols), jnp.float32),
            pltpu.VMEM((eig_cols, eig_cols), jnp.float32),
            pltpu.SemaphoreType.DMA((2,)),
        ],
        compiler_params=pltpu.CompilerParams(vmem_limit_bytes=40 * 1024 * 1024),
        cost_estimate=pl.CostEstimate(
            flops=2 * total_rows * total_rows * (width + 6 * eig_cols),
            bytes_accessed=2 * total_rows * (width + 2 * eig_cols),
            transcendentals=total_rows * total_rows,
        ),
        name="subspace_sweeps",
    )(*pieces)


def replicated(particles, start_basis):
    shard_rows, width = particles.shape
    eig_cols = start_basis.shape[1]
    base_hi = lax.reduce_precision(start_basis, 8, 7)
    base_lo = lax.reduce_precision(start_basis - base_hi, 8, 7)
    packed = jnp.concatenate(
        [particles, base_hi.astype(jnp.bfloat16), base_lo.astype(jnp.bfloat16)], axis=1
    )
    return whole(gather_all(packed), shard_rows, width, eig_cols)


def local(particles, start_basis):
    devices = lax.axis_size("row") * lax.axis_size("col") * lax.axis_size("vec")
    if particles.shape[0] * devices <= WHOLE_ROWS:
        return replicated(particles, start_basis)
    return sharded(particles, start_basis)


def solution(mesh):
    placed = (P(AXES, None), P(AXES, None))
    return jax.shard_map(
        local,
        mesh=mesh,
        in_specs=placed,
        out_specs=(P(AXES, None), P()),
        check_vma=False,
    )
```
